512 devices in a mesh: ep: 64 (over y, z), tp: 8 (over x, core).
Axes of the slice: x: 4, y: 4, z: 16, core: 2. Of those that a mesh axis runs over, the one named last changes fastest.
Arguments:
- tokens: bfloat16 [8192, 4096], P('ep', 'tp'), may hold values from -6 to 6
- routes: int32 [8192, 8], P('ep'), may hold values from 0 to 127, as said below
- gates: float32 [8192, 8], P('ep'), may hold values from 0.02 to 0.5
- up_weight: bfloat16 [128, 4096, 1024], P('ep', 'tp'), may hold values from -0.09375 to 0.09375
- replica_on: int32 [128], replicated, may hold values from 0 to 1, as said below
- grad_out: bfloat16 [8192, 1024], P('ep', 'tp'), may hold values from -6 to 6
Outputs:
- mixed: bfloat16 [8192, 1024], P('ep', 'tp')
- grad_tokens: bfloat16 [8192, 4096], P('ep', 'tp')
- grad_gates: float32 [8192, 8], P('ep')
- grad_up: bfloat16 [128, 4096, 1024], P('ep', 'tp')
The draws below stay inside these ranges and needn't reach their ends.
Inputs may be any that keep to these rules, and one draw needn't show every extreme that they name: `routes`: each row names 8 different experts; every expert is named by some row. `replica_on`: of the experts j * 2 to (j + 1) * 2 - 1, exactly one has value 1, for every j.
All inputs are finite; a program needn't handle non-finite values.
Results may differ from the reference program's by a relative error of at most 0.0095.
Values may be sent and summed in bfloat16 or wider, within the bound.
A program may use at most 64 MiB of HBM per device.

```python
import math
import jax
import jax.numpy as jnp
from jax import lax

D = 4096
FF = 1024
TOPK = 8
EXP_DEV = 2
TOK_EP = 128
EXPERTS = 128
TOKENS = 8192
CAP = 6
N_EP = 64


def replica_plan(key):
    picks = jax.random.randint(key, (EXPERTS // EXP_DEV,), 0, EXP_DEV, dtype=jnp.int32)
    expanded = jnp.repeat(picks, EXP_DEV)
    within = jnp.arange(EXPERTS, dtype=jnp.int32) % EXP_DEV
    return within == expanded


def draw_routes(key, part):
    chosen = replica_plan(key)
    key = jax.random.fold_in(key, 3)
    weights = jnp.where(chosen, 4, 1).astype(jnp.int32)
    draws = jax.random.randint(key, (TOKENS, EXPERTS), 0, 65536, dtype=jnp.int32)
    experts_row = jnp.arange(EXPERTS, dtype=jnp.int32)
    scores = draws * weights[None, :] * EXPERTS + experts_row[None, :]
    first = jnp.arange(TOKENS, dtype=jnp.int32) % EXPERTS
    scores = jnp.where(experts_row[None, :] == first[:, None], -1, scores)
    unused, others = lax.top_k(scores, TOPK - 1)
    return jnp.concatenate([first[:, None], others.astype(jnp.int32)], 1)


def draw_replica_on(key, part):
    chosen = replica_plan(key)
    return chosen.astype(jnp.int32)


def levels(rng, dims, pieces, least, top_value):
    level, own = 1.0, jax.random.fold_in(rng, 6)
    for axis_at, shards_of in pieces:
        heights = jnp.exp(jax.random.uniform(jax.random.fold_in(own, axis_at), (shards_of,), jnp.float32, least / len(pieces), top_value / len(pieces)))
        level = level * jnp.repeat(heights, dims[axis_at] // shards_of).reshape([-1 if axis == axis_at else 1 for axis in range(len(dims))])
    return level


def bell_draw(key, shape, width, limit, pieces=(), held_as=jnp.bfloat16):
    array = width * jax.random.normal(key, shape, jnp.float32)
    if pieces:
        array = array * levels(key, shape, pieces, -0.22, 0.18)
    return jnp.clip(array, -limit, limit).astype(held_as)


def setup_inputs(seed: int = 0) -> dict:
    key_list = jax.random.split(jax.random.key(seed), 7)
    return {
        "tokens": bell_draw(key_list[0], (TOKENS, D), 1.0, 6.0, ((0, 64), (1, 8))),
        "routes": draw_routes(jax.random.fold_in(key_list[6], 71), 0),
        "gates": jnp.clip(jnp.exp(math.log(0.5) - 3.218876 * jax.random.uniform(key_list[2], (TOKENS, TOPK), jnp.float32) ** levels(key_list[2], (TOKENS, TOPK), ((0, 64),), -0.2, 0.2)), 0.02, 0.5),
        "up_weight": bell_draw(key_list[3], (EXPERTS, D, FF), D ** -0.5, 0.09375, ((0, 64), (1, 8))),
        "replica_on": draw_replica_on(jax.random.fold_in(key_list[6], 71), 0),
        "grad_out": bell_draw(key_list[5], (TOKENS, FF), 1.0, 6.0, ((0, 64), (1, 8))),
    }


def derivative(hidden):
    sig = jax.nn.sigmoid(hidden)
    return sig * (1.0 + hidden * (1.0 - sig))


def reference(tokens, routes, gates, up_weight, replica_on, grad_out):
    groups = N_EP
    per_group = TOK_EP * TOPK
    flat = routes.reshape(groups, per_group)
    onehot = (flat[:, :, None] == jnp.arange(EXPERTS, dtype=jnp.int32)[None, None, :]).astype(jnp.int32)
    before = jnp.cumsum(onehot, 1) - onehot
    rank = jnp.sum(before * onehot, 2)
    copies = 1 + replica_on[flat]
    copy_index = rank % copies
    slot = rank // copies
    kept = slot < CAP
    group_index = jnp.arange(groups, dtype=jnp.int32)[:, None]
    total = EXPERTS * groups * 2 * CAP
    position = jnp.where(kept, ((flat * groups + group_index) * 2 + copy_index) * CAP + slot, total).astype(jnp.int32)
    pair_ids = jnp.arange(TOKENS * TOPK, dtype=jnp.int32).reshape(groups, per_group)
    table = jnp.full((total + 1,), TOKENS * TOPK, dtype=jnp.int32)
    table = table.at[position.reshape(-1)].set(pair_ids.reshape(-1))[:total].reshape(EXPERTS, groups * 2 * CAP)
    padded_x = jnp.concatenate([tokens, jnp.zeros((1, D), tokens.dtype)], 0)
    row_grad = (gates[:, :, None] * grad_out[:, None, :].astype(jnp.float32)).astype(jnp.bfloat16)
    padded_g = jnp.concatenate([row_grad.reshape(TOKENS * TOPK, FF), jnp.zeros((1, FF), jnp.bfloat16)], 0)

    def per_expert(operands):
        index, w_up = operands
        inputs = padded_x[index // TOPK]
        grads = padded_g[index]
        hidden = jnp.dot(inputs, w_up, preferred_element_type=jnp.float32)
        act = jax.nn.silu(hidden).astype(jnp.bfloat16)
        hidden_grad = (grads.astype(jnp.float32) * derivative(hidden)).astype(jnp.bfloat16)
        g_up = jnp.dot(inputs.T, hidden_grad, preferred_element_type=jnp.float32).astype(jnp.bfloat16)
        input_grad = jnp.dot(hidden_grad, w_up.T, preferred_element_type=jnp.float32).astype(jnp.bfloat16)
        return act, input_grad, g_up

    act, input_grad, grad_up = lax.map(per_expert, (table, up_weight))
    where = position.reshape(TOKENS, TOPK)
    act_flat = jnp.concatenate([act.reshape(total, FF), jnp.zeros((1, FF), jnp.bfloat16)], 0)
    act_pairs = act_flat[where].astype(jnp.float32)
    mixed = jnp.einsum("tk,tkf->tf", gates, act_pairs).astype(jnp.bfloat16)
    grad_gates = jnp.einsum("tkf,tf->tk", act_pairs, grad_out.astype(jnp.float32))
    input_flat = jnp.concatenate([input_grad.reshape(total, D), jnp.zeros((1, D), jnp.bfloat16)], 0)
    grad_tokens = jnp.sum(input_flat[where].astype(jnp.float32), 1).astype(jnp.bfloat16)
    return mixed, grad_tokens, grad_gates, grad_up
```

```python
import jax
import jax.numpy as jnp
from jax import lax
from jax.sharding import PartitionSpec as P

CAP = 6
ROWS = 3 * CAP


def derivative(hidden):
    sig = jax.nn.sigmoid(hidden)
    return sig * (1.0 + hidden * (1.0 - sig))


def exact_dot(a, b):
    return jnp.dot(a, b, preferred_element_type=jnp.float32)


def on_device(tokens, routes, gates, up_weight, replica_on, grad_out):
    count, feat = tokens.shape
    topk = routes.shape[1]
    experts = replica_on.shape[0]
    n_ep = lax.axis_size("ep")
    total = n_ep * ROWS
    share = grad_out.shape[1]
    choice = routes[:, :, None] == jnp.arange(experts, dtype=jnp.int32)[None, None, :]
    names = jnp.sum(choice.astype(jnp.float32), 1)
    lower = jnp.tril(jnp.ones((count, count), jnp.bfloat16), -1)
    rank = exact_dot(lower, names.astype(jnp.bfloat16)).astype(jnp.int32)
    kept = rank < CAP * (1 + replica_on)[None, :]
    expert_ids = jnp.arange(experts, dtype=jnp.int32)
    base = (expert_ids // 2) * ROWS + jnp.where(replica_on == 1, 0, 2 * CAP)
    place = jnp.where(kept, rank + base[None, :], -1)
    position = jnp.sum(jnp.where(choice, place[:, None, :], 0), 2)
    row_ids = jnp.arange(total, dtype=jnp.int32)
    match = position[None, :, :] == row_ids[:, None, None]
    pick = jnp.any(match, 2).astype(jnp.bfloat16)
    gate_row = jnp.sum(jnp.where(match, gates[None, :, :], 0.0), (1, 2))
    sent = exact_dot(pick, tokens).astype(jnp.bfloat16).reshape(n_ep, ROWS, feat)
    grad_rows = exact_dot(pick, grad_out)
    sent_grads = (gate_row[:, None] * grad_rows).astype(jnp.bfloat16).reshape(n_ep, ROWS, share)
    received = lax.all_to_all(sent, "ep", split_axis=0, concat_axis=0, tiled=True)
    x_hot = received[:, : 2 * CAP].reshape(n_ep * 2 * CAP, feat)
    x_cold = received[:, 2 * CAP :].reshape(n_ep * CAP, feat)
    grads_in = lax.all_to_all(sent_grads, "ep", split_axis=0, concat_axis=0, tiled=True)
    hot_is_1 = replica_on[2 * lax.axis_index("ep") + 1] == 1
    w_hot = jnp.where(hot_is_1, up_weight[1], up_weight[0])
    w_cold = jnp.where(hot_is_1, up_weight[0], up_weight[1])
    partial_value = jnp.concatenate([exact_dot(x_hot, w_hot), exact_dot(x_cold, w_cold)], 0)
    hidden = lax.psum_scatter(partial_value, "tp", scatter_dimension=1, tiled=True)
    n_hot = n_ep * 2 * CAP

    def by_group(rows):
        return jnp.concatenate(
            [rows[:n_hot].reshape(n_ep, 2 * CAP, -1), rows[n_hot:].reshape(n_ep, CAP, -1)], 1
        )

    act = jax.nn.silu(hidden).astype(jnp.bfloat16)
    grads_flat = jnp.concatenate(
        [grads_in[:, : 2 * CAP].reshape(n_hot, share), grads_in[:, 2 * CAP :].reshape(-1, share)], 0
    )
    grad_part = (grads_flat.astype(jnp.float32) * derivative(hidden)).astype(jnp.bfloat16)
    hidden_grad = lax.all_gather(grad_part, "tp", axis=1, tiled=True)
    returned = lax.all_to_all(by_group(act), "ep", split_axis=0, concat_axis=0, tiled=True)
    returned = returned.reshape(total, share).astype(jnp.float32)
    mixed = lax.dot_general(
        pick.astype(jnp.float32),
        gate_row[:, None] * returned,
        (((0,), (0,)), ((), ())),
        precision=lax.Precision.HIGHEST,
        preferred_element_type=jnp.float32,
    ).astype(jnp.bfloat16)
    gate_part = jnp.sum(returned * grad_rows, 1)
    gate_pairs = jnp.sum(jnp.where(match, gate_part[:, None, None], 0.0), 0)
    grad_gates = lax.psum(gate_pairs, "tp")
    contract_f = (((1,), (1,)), ((), ()))
    back_hot = lax.dot_general(hidden_grad[:n_hot], w_hot, contract_f, preferred_element_type=jnp.float32)
    back_cold = lax.dot_general(hidden_grad[n_hot:], w_cold, contract_f, preferred_element_type=jnp.float32)
    input_rows = by_group(jnp.concatenate([back_hot, back_cold], 0).astype(jnp.bfloat16))
    back = lax.all_to_all(input_rows, "ep", split_axis=0, concat_axis=0, tiled=True).reshape(total, feat)
    contract_r = (((0,), (0,)), ((), ()))
    grad_tokens = lax.dot_general(pick, back, contract_r, preferred_element_type=jnp.float32).astype(jnp.bfloat16)
    g_hot = lax.dot_general(x_hot, hidden_grad[:n_hot], contract_r, preferred_element_type=jnp.float32)
    g_cold = lax.dot_general(x_cold, hidden_grad[n_hot:], contract_r, preferred_element_type=jnp.float32)
    grad_up = jnp.stack(
        [jnp.where(hot_is_1, g_cold, g_hot), jnp.where(hot_is_1, g_hot, g_cold)]
    ).astype(jnp.bfloat16)
    return (mixed, grad_tokens, grad_gates, grad_up)


def solution(mesh):
    return jax.shard_map(
        on_device,
        mesh=mesh,
        in_specs=(
            P("ep", "tp"),
            P("ep", None),
            P("ep", None),
            P("ep", "tp", None),
            P(),
            P("ep", "tp"),
        ),
        out_specs=(P("ep", "tp"), P("ep", "tp"), P("ep", None), P("ep", "tp", None)),
        check_vma=False,
    )
```

```python
import functools

import jax
import jax.numpy as jnp
from jax import lax
from jax.experimental import pallas as pl
from jax.experimental.pallas import tpu as pltpu
from jax.sharding import PartitionSpec as P

MESH = pl.DeviceIdType.MESH
CAP = 6
CAPS = (2 * CAP, CAP)
NY = 4
BF16, F32 = jnp.bfloat16, jnp.float32


def dot(a, b, ca=1, cb=0):
    return lax.dot_general(a, b, (((ca,), (cb,)), ((), ())), preferred_element_type=F32)


def two_parts(value):
    high = value.astype(BF16)
    return high, (value - high.astype(F32)).astype(BF16)


def kernel(
    dims,
    info_ref, eid_ref, hot_ref, tokens_ref, grad_ref, weight_hbm,
    mixed_ref, gtok_ref, ggate_ref, gup_hbm,
    ring, inf, wraw, wsel, pmat, gatec, graw, xsend, xin, part, pin, psend, precv,
    act, aret, hgown, hg, brow, rret, ptok, rs, pmix, ms, pgg, gs, gup, gx,
    wsem, osem, lsem, ag, agi, ysem, csem, xsem, asem, hxsem, hcsem, bsem, rsem, msem, gsem, txsem,
):
    ny, nz, nx, topk = dims
    count, feat = tokens_ref.shape
    share = grad_ref.shape[1]
    ff = wsel.shape[2]
    half = nz // 2
    off = nz // 4 - 1
    nslot = nz // 2
    hrow, crow = CAPS[0] * nslot, CAPS[1] * nslot
    spans = [
        (j, h, (j * hrow if h == 0 else ny * hrow + j * crow), (hrow, crow)[h])
        for h in range(2)
        for j in range(ny)
    ]
    whole = [(0, ny * hrow), (ny * hrow, ny * crow)]
    rows = ny * (hrow + crow)
    t2 = count // 2

    ep, tp = lax.axis_index("ep"), lax.axis_index("tp")
    y, z = lax.div(ep, nz), lax.rem(ep, nz)
    x, c = lax.div(tp, 2), lax.rem(tp, 2)

    def device(yy, zz, xx, cc):
        return (lax.rem(yy, ny) * nz + lax.rem(zz, nz), lax.rem(xx, nx) * 2 + cc)

    z_to = (device(y, z + nz - 1, x, c), device(y, z + 1, x, c))
    y_to = [device(y + j, z, x, c) for j in range(ny)]
    y_back = [device(y + ny - j, z, x, c) for j in range(ny)]
    x_to = [device(y, z, x + i, c) for i in range(nx)]
    other = device(y, z, x, 1 - c)

    def pos(d):
        return (d + off) % nz

    def send(src, dst, sems, to):
        return pltpu.make_async_remote_copy(
            src_ref=src, dst_ref=dst, send_sem=sems.at[0], recv_sem=sems.at[1],
            device_id=to, device_id_type=MESH,
        )

    load = pltpu.make_async_copy(weight_hbm, wraw, wsem)
    load.start()
    barrier = pltpu.get_barrier_semaphore()
    partners = list(z_to) + y_to[1:] + x_to[1:] + [other]
    for partner in partners:
        pl.semaphore_signal(barrier, inc=1, device_id=partner, device_id_type=MESH)
    pl.semaphore_wait(barrier, len(partners))

    mine = pos(0) * count
    ring[mine : mine + count, :feat] = tokens_ref[...]
    ring[mine : mine + count, feat:] = grad_ref[...]
    inf[pos(0)] = info_ref[...]

    sign = (1, -1)

    def ag_copy(way, s, h):
        src, dst = pos(sign[way] * (s - 1)), pos(sign[way] * s)
        return send(
            ring.at[pl.ds(src * count + h * t2, t2)], ring.at[pl.ds(dst * count + h * t2, t2)],
            ag.at[way, s - 1, h], z_to[way],
        )

    def ag_info(way, s):
        src, dst = pos(sign[way] * (s - 1)), pos(sign[way] * s)
        return send(inf.at[src], inf.at[dst], agi.at[way, s - 1], z_to[way])

    def ag_has(way, s, h):
        return s < half or (s == half and h == way)

    def ag_info_has(way, s):
        return s < half or (s == half and way == 0)

    upper = (
        lax.broadcasted_iota(jnp.int32, (count, count), 0)
        < lax.broadcasted_iota(jnp.int32, (count, count), 1)
    ).astype(BF16)

    def y_copy(b, k, sems, src, dst, to):
        j, h, r0, n = spans[k]
        return send(src.at[b, pl.ds(r0, n)], dst.at[b, pl.ds(r0, n)], sems.at[b, k], to[j])

    def y_copies(b, sems, src, dst, to):
        return [y_copy(b, k, sems, src, dst, to) for k in range(len(spans)) if spans[k][0] > 0]

    def gather(b):
        eids = eid_ref[...]
        caps = jnp.where(lax.broadcasted_iota(jnp.int32, eids.shape, 0) % 2 == 0, CAPS[0], CAPS[1])
        caps = caps.astype(F32)
        names, gate_of = [], []
        for g in range(nslot):
            named = jnp.zeros(eids.shape, F32)
            gated = jnp.zeros(eids.shape, F32)
            block = inf[b * nslot + g]
            for k in range(topk):
                hit = block[k : k + 1] == eids
                named = named + jnp.where(hit, 1.0, 0.0)
                gated = gated + jnp.where(hit, block[topk + k : topk + k + 1], 0.0)
            names.append(named)
            gate_of.append(gated)
        rank = dot(jnp.concatenate(names, 0).astype(BF16), upper)
        place = []
        for g in range(nslot):
            r = rank[g * 2 * ny : (g + 1) * 2 * ny]
            place.append(jnp.where((names[g] > 0.0) & (r < caps), r + g * caps, -1.0))
        place = jnp.concatenate(place, 1)
        gate_of = jnp.concatenate(gate_of, 1)
        for j, h, r0, n in spans:
            e = 2 * j + h
            at = lax.broadcasted_iota(jnp.int32, (n, nslot * count), 0).astype(F32)
            hit = at == place[e : e + 1]
            pmat[b, r0 : r0 + n] = jnp.where(hit, 1.0, 0.0).astype(BF16)
            gate = jnp.sum(jnp.where(hit, gate_of[e : e + 1], 0.0), 1, keepdims=True)
            gatec[b, r0 : r0 + n] = jnp.broadcast_to(gate, (n, share))
        pick = pmat[b]
        base = b * nslot * count
        for c0 in range(0, feat, min(256, feat)):
            cols = slice(c0, c0 + min(256, feat))
            got = dot(pick, ring[base : base + nslot * count, cols]).astype(BF16)
            xsend[b, :, cols] = got
            xin[b, 0:hrow, cols] = got[0:hrow]
            xin[b, ny * hrow : ny * hrow + crow, cols] = got[ny * hrow : ny * hrow + crow]
        got = dot(pick, ring[base : base + nslot * count, feat:])
        graw[b] = got.astype(BF16)
        row_grad = (gatec[b] * got).astype(BF16)
        xsend[b, :, feat:] = row_grad
        xin[b, 0:hrow, feat:] = row_grad[0:hrow]
        xin[b, ny * hrow : ny * hrow + crow, feat:] = row_grad[ny * hrow : ny * hrow + crow]
        for copy in y_copies(b, ysem, xsend, xin, y_to):
            copy.start()

    def core_copy(b):
        return send(part.at[b, 1 - c], pin.at[b], csem.at[b], other)

    def forward(b):
        for copy in y_copies(b, ysem, xsend, xin, y_to):
            copy.wait_recv()
        for h, (r0, n) in enumerate(whole):
            rows_in = xin[b, r0 : r0 + n, :feat]
            for t in range(0, ff // share, 2):
                out = dot(rows_in, wsel[h, :, t * share : (t + 2) * share]).astype(BF16)
                part[b, 0, t // 2, r0 : r0 + n] = out[:, :share]
                part[b, 1, t // 2, r0 : r0 + n] = out[:, share:]
        core_copy(b).start()

    def x_copy(b, i):
        return send(psend.at[b, i], precv.at[b, i], xsem.at[b, i], x_to[i])

    def pair_sum(b):
        core_copy(b).wait_recv()
        for i in [*range(1, nx), 0]:
            to = lax.rem(x + i, nx)
            total = part[b, c, to].astype(F32) + pin[b, to].astype(F32)
            psend[b, i] = total.astype(BF16)
            if i > 0:
                x_copy(b, i).start()

    def strip(b, t):
        return hg.at[b, :, pl.ds(pl.multiple_of(t * share, share), share)]

    def hg_x(b, i):
        return send(hgown.at[b], strip(b, tp), hxsem.at[b, i], x_to[i])

    def hg_core(b, i):
        t = lax.rem(x + nx - i, nx) * 2 + c
        return send(hgown.at[b] if i == 0 else strip(b, t), strip(b, t), hcsem.at[b, i], other)

    def hg_keep(b):
        return pltpu.make_async_copy(hgown.at[b], strip(b, tp), lsem.at[b])

    def middle(b):
        hidden = psend[b, 0].astype(F32)
        for i in range(1, nx):
            x_copy(b, i).wait_recv()
            hidden = hidden + precv[b, i].astype(F32)
        sig = jax.nn.sigmoid(hidden)
        row_grad = xin[b, :, feat:].astype(F32)
        hgown[b] = (row_grad * (sig * (1.0 + hidden * (1.0 - sig)))).astype(BF16)
        for i in range(1, nx):
            hg_x(b, i).start()
        hg_core(b, 0).start()
        hg_keep(b).start()
        acts = (hidden * sig).astype(BF16)
        act[b] = acts
        aret[b, 0:hrow] = acts[0:hrow]
        aret[b, ny * hrow : ny * hrow + crow] = acts[ny * hrow : ny * hrow + crow]
        for copy in y_copies(b, asem, act, aret, y_back):
            copy.start()

    def hg_forward(b):
        for i in range(1, nx):
            hg_x(b, i).wait_recv()
            hg_core(b, i).start()

    def mix(b):
        for copy in y_copies(b, asem, act, aret, y_back):
            copy.wait_recv()
        acts = aret[b].astype(F32)
        base = b * nslot * count
        weighted = (gatec[b] * acts).astype(BF16)
        pmix[base : base + nslot * count] = dot(pmat[b], weighted, 0, 0).astype(BF16)
        high, low = two_parts(acts * graw[b].astype(F32))
        ones = jnp.ones((8, share), BF16)
        sums = []
        for j, h, r0, n in spans:
            line = dot(ones, high[r0 : r0 + n], 1, 1) + dot(ones, low[r0 : r0 + n], 1, 1)
            line_high, line_low = two_parts(line)
            spread = pmat[b, r0 : r0 + n]
            sums.append((2 * j + h, dot(line_high, spread) + dot(line_low, spread)))
        for g in range(nslot):
            named = inf[b * nslot + g, :topk]
            out = jnp.zeros((topk, count), F32)
            for e, value in sums:
                here = value[:topk, g * count : (g + 1) * count]
                out = out + jnp.where(named == eid_ref[e : e + 1], here, 0.0)
            pgg[b * nslot + g] = out

    def backward(b):
        hg_keep(b).wait()
        for i in range(nx):
            hg_core(b, i).wait_recv()
        for h, (r0, n) in enumerate(whole):
            out = dot(hg[b, r0 : r0 + n], wsel[h], 1, 1).astype(BF16)
            brow[b, r0 : r0 + n] = out
            own = (hrow, crow)[h]
            rret[b, r0 : r0 + own] = out[0:own]
        for copy in y_copies(b, bsem, brow, rret, y_back):
            copy.start()

    def scatter(b):
        for copy in y_copies(b, bsem, brow, rret, y_back):
            copy.wait_recv()
        base = b * nslot * count
        ptok[base : base + nslot * count] = dot(pmat[b], rret[b], 0, 0).astype(BF16)

    def weight_grad(k):
        wide = ff // 4
        cols = slice(k * wide, (k + 1) * wide)
        sums = []
        for r0, n in whole:
            total = dot(xin[0, r0 : r0 + n, :feat], hg[0, r0 : r0 + n, cols], 0, 0)
            sums.append(total + dot(xin[1, r0 : r0 + n, :feat], hg[1, r0 : r0 + n, cols], 0, 0))
        swap = hot_ref[:, cols] > 0.0
        gup[0, :, cols] = jnp.where(swap, sums[1], sums[0]).astype(BF16)
        gup[1, :, cols] = jnp.where(swap, sums[0], sums[1]).astype(BF16)

    def rs_copy(way, d, h):
        src = pos(sign[1 - way] * d) * count + h * t2
        return send(
            ptok.at[pl.ds(src, t2)], rs.at[way, d - 1, pl.ds(h * t2, t2)],
            rsem.at[way, d - 1, h], z_to[way],
        )

    def rs_has(way, d, h):
        return d < half or (d == half and h == 1 - way)

    def rs_start(d):
        for way, h in ((1, 0), (0, 1), (1, 1), (0, 0)):
            if d == half and not rs_has(way, d, h):
                continue
            if rs_has(way, d + 1, h) and d < half:
                continue
            rs_copy(way, d, h).start()

    def rs_step(d):
        for h in range(2):
            for way in (1, 0):
                if not rs_has(way, d + 1, h):
                    continue
                rs_copy(way, d + 1, h).wait_recv()
                at = pos(sign[1 - way] * d) * count + h * t2
                arrived = rs[way, d, h * t2 : (h + 1) * t2].astype(F32)
                ptok[at : at + t2] = (ptok[at : at + t2].astype(F32) + arrived).astype(BF16)
                rs_copy(way, d, h).start()

    def rs_end():
        for h in range(2):
            total = ptok[mine + h * t2 : mine + (h + 1) * t2].astype(F32)
            for way in (1, 0):
                rs_copy(way, 1, h).wait_recv()
                total = total + rs[way, 0, h * t2 : (h + 1) * t2].astype(F32)
            gtok_ref[h * t2 : (h + 1) * t2] = total.astype(BF16)

    def ms_copy(way, d):
        src = pos(sign[1 - way] * d)
        return send(
            pmix.at[pl.ds(src * count, count)], ms.at[way, d - 1], msem.at[way, d - 1], z_to[way]
        )

    def gs_copy(way, d):
        src = pos(sign[1 - way] * d)
        return send(pgg.at[src], gs.at[way, d - 1], gsem.at[way, d - 1], z_to[way])

    def ms_has(way, d):
        return d < half or (d == half and way == 1)

    def ms_step(d):
        for way in (1, 0):
            if not ms_has(way, d):
                continue
            if ms_has(way, d + 1):
                src = pos(sign[1 - way] * d)
                ms_copy(way, d + 1).wait_recv()
                at = slice(src * count, (src + 1) * count)
                pmix[at] = (pmix[at].astype(F32) + ms[way, d].astype(F32)).astype(BF16)
                gs_copy(way, d + 1).wait_recv()
                pgg[src] = pgg[src] + gs[way, d]
            ms_copy(way, d).start()
            gs_copy(way, d).start()

    def tx_core():
        return send(gx.at[0], gx.at[1], txsem.at[0], other)

    def tx_copy(i):
        return send(gx.at[2], gx.at[2 + i], txsem.at[i], x_to[i])

    def ms_end():
        total = pmix[mine : mine + count].astype(F32)
        gates = pgg[pos(0)]
        for way in (1, 0):
            ms_copy(way, 1).wait_recv()
            total = total + ms[way, 0].astype(F32)
            gs_copy(way, 1).wait_recv()
            gates = gates + gs[way, 0]
        mixed_ref[...] = total.astype(BF16)
        gx[0] = gates
        tx_core().start()

    def tx_middle():
        tx_core().wait_recv()
        gx[2] = gx[0] + gx[1]
        for i in range(1, nx):
            tx_copy(i).start()

    def tx_end():
        total = gx[2]
        for i in range(1, nx):
            tx_copy(i).wait_recv()
            total = total + gx[2 + i]
        ggate_ref[...] = total

    def order_weights():
        load.wait()
        for k in range(4):
            cols = slice(k * (ff // 4), (k + 1) * (ff // 4))
            swap = hot_ref[:, cols] > 0.0
            first, second = wraw[0, :, cols].astype(F32), wraw[1, :, cols].astype(F32)
            wsel[0, :, cols] = jnp.where(swap, second, first).astype(BF16)
            wsel[1, :, cols] = jnp.where(swap, first, second).astype(BF16)

    for way in (0, 1):
        ag_info(way, 1).start()
    for h in range(2):
        for way in (0, 1):
            ag_copy(way, 1, h).start()
    early = [order_weights]
    ready = nz // 4
    stages = [
        functools.partial(gather, 0), functools.partial(forward, 0),
        functools.partial(pair_sum, 0), functools.partial(middle, 0),
        functools.partial(hg_forward, 0), functools.partial(mix, 0),
        functools.partial(backward, 0), functools.partial(scatter, 0),
    ]
    done = 0
    for s in range(1, half + 1):
        for way in (0, 1):
            if ag_info_has(way, s):
                ag_info(way, s).wait_recv()
                if ag_info_has(way, s + 1):
                    ag_info(way, s + 1).start()
        for h in range(2):
            for way in (0, 1):
                if ag_has(way, s, h):
                    ag_copy(way, s, h).wait_recv()
                    if ag_has(way, s + 1, h):
                        ag_copy(way, s + 1, h).start()
        if s == 1:
            order_weights()
        if ready <= s < half:
            stages[done]()
            done += 1
    late = [
        functools.partial(gather, 1), functools.partial(forward, 1),
        functools.partial(pair_sum, 1), functools.partial(middle, 1),
    ]
    for stage in late:
        stage()
        if done < len(stages):
            stages[done]()
            done += 1
    while done < len(stages):
        stages[done]()
        done += 1
    hg_forward(1)
    mix(1)
    steps = list(range(half, 0, -1))
    for d in steps[:2]:
        ms_step(d)
    backward(1)
    for d in steps[2:5]:
        ms_step(d)
    scatter(1)
    rest = [functools.partial(ms_step, d) for d in steps[5:]] + [ms_end, tx_middle, tx_end]
    rest = rest + [functools.partial(weight_grad, k) for k in range(4)]
    rs_start(half)
    if half > 1:
        rs_start(half - 1)
    for d in range(half - 1, 0, -1):
        rs_step(d)
        for _ in range(2):
            if rest:
                rest.pop(0)()
    for job in rest:
        job()
    store = pltpu.make_async_copy(gup, gup_hbm, osem)
    store.start()
    rs_end()
    store.wait()

    for s in range(1, half + 1):
        for way in (0, 1):
            if ag_info_has(way, s):
                ag_info(way, s).wait_send()
            for h in range(2):
                if ag_has(way, s, h):
                    ag_copy(way, s, h).wait_send()
                if rs_has(way, s, h):
                    rs_copy(way, s, h).wait_send()
            if ms_has(way, s):
                ms_copy(way, s).wait_send()
                gs_copy(way, s).wait_send()
    for b in range(2):
        for copy in y_copies(b, ysem, xsend, xin, y_to):
            copy.wait_send()
        for copy in y_copies(b, asem, act, aret, y_back):
            copy.wait_send()
        for copy in y_copies(b, bsem, brow, rret, y_back):
            copy.wait_send()
        core_copy(b).wait_send()
        for i in range(nx):
            hg_core(b, i).wait_send()
            if i > 0:
                x_copy(b, i).wait_send()
                hg_x(b, i).wait_send()
    tx_core().wait_send()
    for i in range(1, nx):
        tx_copy(i).wait_send()


def on_device(ny, tokens, routes, gates, up_weight, replica_on, grad_out):
    count, feat = tokens.shape
    topk = routes.shape[1]
    share = grad_out.shape[1]
    ff = up_weight.shape[2]
    experts = replica_on.shape[0]
    nz = lax.axis_size("ep") // ny
    nx = lax.axis_size("tp") // 2
    me = lax.axis_index("ep")
    info = jnp.concatenate([routes.T.astype(F32), gates.T], 0)
    line = jnp.arange(2 * ny, dtype=jnp.int32)
    home = ((me // nz + line // 2) % ny) * nz + me % nz
    second = jnp.arange(experts, dtype=jnp.int32)[None, :] == (2 * home + 1)[:, None]
    second = jnp.sum(jnp.where(second, replica_on[None, :], 0), 1)
    eids = 2 * home + jnp.where(line % 2 == 0, second, 1 - second)
    eids = jnp.broadcast_to(eids.astype(F32)[:, None], (2 * ny, count))
    hot = jnp.broadcast_to(second[0].astype(F32), (1, ff))

    half = nz // 2
    rows = ny * half * 3 * CAP
    slots = half * count
    vmem = pl.BlockSpec(memory_space=pltpu.VMEM)
    hbm = pl.BlockSpec(memory_space=pl.ANY)

    def dma(*shape):
        return pltpu.SemaphoreType.DMA(shape + (2,))

    mixed, gtok, ggate, gup = pl.pallas_call(
        functools.partial(kernel, (ny, nz, nx, topk)),
        out_shape=[
            jax.ShapeDtypeStruct((count, share), BF16),
            jax.ShapeDtypeStruct((count, feat), BF16),
            jax.ShapeDtypeStruct((topk, count), F32),
            jax.ShapeDtypeStruct(up_weight.shape, BF16),
        ],
        in_specs=[vmem] * 5 + [hbm],
        out_specs=[vmem] * 3 + [hbm],
        scratch_shapes=[
            pltpu.VMEM((nz * count, feat + share), BF16),
            pltpu.VMEM((nz, 2 * topk, count), F32),
            pltpu.VMEM(up_weight.shape, BF16),
            pltpu.VMEM(up_weight.shape, BF16),
            pltpu.VMEM((2, rows, slots), BF16),
            pltpu.VMEM((2, rows, share), F32),
            pltpu.VMEM((2, rows, share), BF16),
            pltpu.VMEM((2, rows, feat + share), BF16),
            pltpu.VMEM((2, rows, feat + share), BF16),
            pltpu.VMEM((2, 2, nx, rows, share), BF16),
            pltpu.VMEM((2, nx, rows, share), BF16),
            pltpu.VMEM((2, nx, rows, share), BF16),
            pltpu.VMEM((2, nx, rows, share), BF16),
            pltpu.VMEM((2, rows, share), BF16),
            pltpu.VMEM((2, rows, share), BF16),
            pltpu.VMEM((2, rows, share), BF16),
            pltpu.VMEM((2, rows, ff), BF16),
            pltpu.VMEM((2, rows, feat), BF16),
            pltpu.VMEM((2, rows, feat), BF16),
            pltpu.VMEM((nz * count, feat), BF16),
            pltpu.VMEM((2, half, count, feat), BF16),
            pltpu.VMEM((nz * count, share), BF16),
            pltpu.VMEM((2, half, count, share), BF16),
            pltpu.VMEM((nz, topk, count), F32),
            pltpu.VMEM((2, half, topk, count), F32),
            pltpu.VMEM(up_weight.shape, BF16),
            pltpu.VMEM((2 + nx, topk, count), F32),
            pltpu.SemaphoreType.DMA,
            pltpu.SemaphoreType.DMA,
            pltpu.SemaphoreType.DMA((2,)),
            dma(2, half, 2),
            dma(2, half),
            dma(2, 2 * ny),
            dma(2),
            dma(2, nx),
            dma(2, 2 * ny),
            dma(2, nx),
            dma(2, nx),
            dma(2, 2 * ny),
            dma(2, half, 2),
            dma(2, half),
            dma(2, half),
            dma(nx),
        ],
        compiler_params=pltpu.CompilerParams(
            collective_id=0, has_side_effects=True, vmem_limit_bytes=56 * 1024 * 1024
        ),
        cost_estimate=pl.CostEstimate(
            flops=8 * rows * feat * ff, bytes_accessed=8 * feat * ff, transcendentals=2 * rows * share
        ),
    )(info, eids, hot, tokens, grad_out, up_weight)
    return mixed, gtok, ggate.T, gup


def solution(mesh, ny=NY):
    return jax.shard_map(
        functools.partial(on_device, ny),
        mesh=mesh,
        in_specs=(
            P("ep", "tp"), P("ep", None), P("ep", None), P("ep", "tp", None), P(), P("ep", "tp"),
        ),
        out_specs=(P("ep", "tp"), P("ep", "tp"), P("ep", None), P("ep", "tp", None)),
        check_vma=False,
    )
```

```python
import functools

import jax
import jax.numpy as jnp
from jax import lax
from jax.experimental import pallas as pl
from jax.experimental.pallas import tpu as pltpu
from jax.sharding import PartitionSpec as P

MESH = pl.DeviceIdType.MESH
CAP = 6
CAPS = (2 * CAP, CAP)
NY = 4
PIECES = 8
SIZES = (4, 4, 4, 2, 2)
BATCHES = len(SIZES)
BF16, F32 = jnp.bfloat16, jnp.float32


def dot(a, b, ca=1, cb=0):
    return lax.dot_general(a, b, (((ca,), (cb,)), ((), ())), preferred_element_type=F32)


def two_parts(value):
    high = value.astype(BF16)
    return high, (value - high.astype(F32)).astype(BF16)


def slot_order(nz):
    order = [0]
    for far in range(1, nz // 2):
        order += [far, nz - far]
    return order + [nz // 2]


def block_rows(nslot):
    return tuple(-(-cap * nslot // 16) * 16 for cap in CAPS)


DURING = {
    (2, 3): "g0", (4, 2): "f0", (4, 3): "g1", (5, 0): "p0", (6, 1): "m0", (6, 2): "f1",
    (6, 3): "g2", (7, 0): "p1", (7, 2): "h0", (7, 3): "g3", (8, 0): "b0", (8, 1): "m1 f2",
    (8, 3): "g4",
}
BETWEEN = (
    "p2 f3 x0 p3 s0 f4 h1 x1 p4 m2 m3 b1 m4 h2 x2 x3 h3 b2 b3 s1 x4 M8 h4 M7 b4 M6 s3 M5 s4"
)


def kernel(
    dims,
    routes_ref, gates_ref, rep_ref, tokens_ref, grad_ref, weight_hbm,
    mixed_ref, gtok_ref, ggate_ref, gup_hbm,
    eid, hot, ring, inf, wraw, wsel, pmat, gatec, graw, xsend, xin, part, pin, psend, precv,
    act, aret, hgown, hg, brow, rret, ptok, rs, pmix, ms, pgg, gs, gup, gx,
    wsem, osem, lsem, ag, agi, ysem, csem, xsem, asem, hxsem, hcsem, bsem, rsem, msem, gsem, txsem,
):
    ny, nz, nx = dims
    count, feat = tokens_ref.shape
    topk = routes_ref.shape[0]
    experts = rep_ref.shape[1]
    share = grad_ref.shape[1]
    ff = wsel.shape[2]
    half = nz // 2
    order = slot_order(nz)
    first_slot = [sum(SIZES[:b]) for b in range(BATCHES)]
    pads = [block_rows(size) for size in SIZES]
    blocks_of = [sum(pad) for pad in pads]
    rows_of = [ny * block for block in blocks_of]

    def spans(b):
        return [
            (j, h, j * blocks_of[b] + h * pads[b][0], pads[b][h]) for j in range(ny) for h in range(2)
        ]

    def groups(b):
        return slice(first_slot[b] * count, (first_slot[b] + SIZES[b]) * count)

    quarter = count // 4

    ep, tp = lax.axis_index("ep"), lax.axis_index("tp")
    y, z = lax.div(ep, nz), lax.rem(ep, nz)
    x, c = lax.div(tp, 2), lax.rem(tp, 2)

    def device(yy, zz, xx, cc):
        return (lax.rem(yy, ny) * nz + lax.rem(zz, nz), lax.rem(xx, nx) * 2 + cc)

    z_to = (device(y, z + nz - 1, x, c), device(y, z + 1, x, c))
    y_to = [device(y + j, z, x, c) for j in range(ny)]
    y_back = [device(y + ny - j, z, x, c) for j in range(ny)]
    x_to = [device(y, z, x + i, c) for i in range(nx)]
    other = device(y, z, x, 1 - c)

    def pos(d):
        return order.index(d % nz)

    def send(src, dst, sems, to):
        return pltpu.make_async_remote_copy(
            src_ref=src, dst_ref=dst, send_sem=sems.at[0], recv_sem=sems.at[1],
            device_id=to, device_id_type=MESH,
        )

    load = pltpu.make_async_copy(weight_hbm, wraw, wsem)
    load.start()
    barrier = pltpu.get_barrier_semaphore()
    partners = list(z_to) + y_to[1:] + x_to[1:] + [other]
    for partner in partners:
        pl.semaphore_signal(barrier, inc=1, device_id=partner, device_id_type=MESH)

    mine = pos(0) * count
    ring[mine : mine + count, :feat] = tokens_ref[...]
    ring[mine : mine + count, feat:] = grad_ref[...]
    inf[pos(0), :topk] = routes_ref[...].astype(F32)
    inf[pos(0), topk:] = gates_ref[...]

    def homes(width):
        line = lax.broadcasted_iota(jnp.int32, (2 * ny, width), 0)
        return line, lax.rem(y + lax.shift_right_logical(line, 1), ny) * nz + z

    line, home = homes(experts)
    at = lax.broadcasted_iota(jnp.int32, (2 * ny, experts), 1) == 2 * home + 1
    second = jnp.sum(jnp.where(at, rep_ref[...].astype(F32), 0.0), 1, keepdims=True)
    line, home = homes(count)
    second = jnp.broadcast_to(second, (2 * ny, count))
    eid[...] = 2.0 * home.astype(F32) + jnp.where(lax.rem(line, 2) == 0, second, 1.0 - second)
    hot[...] = second

    def swap(shape):
        return jnp.broadcast_to(hot[0:1, 0:1], shape) > 0.0

    pl.semaphore_wait(barrier, len(partners))

    sign = (1, -1)

    def ag_copy(way, s, q):
        src, dst = pos(sign[way] * (s - 1)) * count, pos(sign[way] * s) * count
        return send(
            ring.at[pl.ds(src + q * quarter, quarter)], ring.at[pl.ds(dst + q * quarter, quarter)],
            ag.at[way, s - 1, q], z_to[way],
        )

    def ag_has(way, s, q):
        return s < half or (s == half and q // 2 == way)

    def ag_info(way, s):
        src, dst = pos(sign[way] * (s - 1)), pos(sign[way] * s)
        return send(inf.at[src], inf.at[dst], agi.at[way, s - 1], z_to[way])

    def ag_info_has(way, s):
        return s < half or (s == half and way == 0)

    def ag_start():
        for q in range(4):
            for way in (0, 1):
                ag_copy(way, 1, q).start()
                if q == 0:
                    ag_info(way, 1).start()

    def ag_step(s, q):
        for way in (0, 1):
            if ag_has(way, s, q):
                ag_copy(way, s, q).wait_recv()
                if ag_has(way, s + 1, q):
                    ag_copy(way, s + 1, q).start()
            if q == 0 and ag_info_has(way, s):
                ag_info(way, s).wait_recv()
                if ag_info_has(way, s + 1):
                    ag_info(way, s + 1).start()

    def blocks(ref, b, h, cols=slice(None)):
        return jnp.concatenate([ref[b, r0 : r0 + n, cols] for j, hh, r0, n in spans(b) if hh == h], 0)

    def y_copies(b, sems, src, dst, to):
        block = blocks_of[b]
        return [
            send(
                src.at[b, pl.ds(j * block, block)], dst.at[b, pl.ds(j * block, block)],
                sems.at[b, j], to[j],
            )
            for j in range(1, ny)
        ]

    def gather(b):
        nslot, rows, block = SIZES[b], rows_of[b], blocks_of[b]
        eids = eid[...]
        caps = lax.rem(lax.broadcasted_iota(jnp.int32, eids.shape, 0), 2) == 0
        caps = jnp.where(caps, float(CAPS[0]), float(CAPS[1]))
        names, gate_of = [], []
        for g in range(nslot):
            named = jnp.zeros(eids.shape, F32)
            gated = jnp.zeros(eids.shape, F32)
            routing = inf[first_slot[b] + g]
            for k in range(topk):
                hit = routing[k : k + 1] == eids
                named = named + jnp.where(hit, 1.0, 0.0)
                gated = gated + jnp.where(hit, routing[topk + k : topk + k + 1], 0.0)
            names.append(named)
            gate_of.append(gated)
        upper = (
            lax.broadcasted_iota(jnp.int32, (count, count), 0)
            < lax.broadcasted_iota(jnp.int32, (count, count), 1)
        ).astype(BF16)
        rank = dot(jnp.concatenate(names, 0).astype(BF16), upper)
        place = []
        for g in range(nslot):
            r = rank[g * 2 * ny : (g + 1) * 2 * ny]
            place.append(jnp.where((names[g] > 0.0) & (r < caps), r + g * caps, -1.0))
        place = jnp.concatenate(place, 1)
        gate_of = jnp.concatenate(gate_of, 1)
        for j, h, r0, n in spans(b):
            e = 2 * j + h
            row = lax.broadcasted_iota(jnp.int32, (n, nslot * count), 0).astype(F32)
            hit = row == place[e : e + 1]
            pmat[b, r0 : r0 + n, : nslot * count] = jnp.where(hit, 1.0, 0.0).astype(BF16)
            gate = jnp.sum(jnp.where(hit, gate_of[e : e + 1], 0.0), 1, keepdims=True)
            gatec[b, r0 : r0 + n] = jnp.broadcast_to(gate, (n, share))
        pick = pmat[b, :rows, : nslot * count]
        for c0 in range(0, feat, min(256, feat)):
            cols = slice(c0, c0 + min(256, feat))
            got = dot(pick, ring[groups(b), cols]).astype(BF16)
            xsend[b, :rows, cols] = got
            xin[b, 0:block, cols] = got[0:block]
        got = dot(pick, ring[groups(b), feat:])
        graw[b, :rows] = got.astype(BF16)
        row_grad = (gatec[b, :rows] * got).astype(BF16)
        xsend[b, :rows, feat:] = row_grad
        xin[b, 0:block, feat:] = row_grad[0:block]
        for copy in y_copies(b, ysem, xsend, xin, y_to):
            copy.start()

    def core_copy(b):
        rows = pl.ds(0, rows_of[b])
        return send(part.at[b, 1 - c, :, rows], pin.at[b, :, rows], csem.at[b], other)

    def forward(b):
        for copy in y_copies(b, ysem, xsend, xin, y_to):
            copy.wait_recv()
        for h in range(2):
            rows_in = blocks(xin, b, h, slice(0, feat))
            for t in range(0, ff // share, 2):
                out = dot(rows_in, wsel[h, :, t * share : (t + 2) * share]).astype(BF16)
                for j, hh, r0, n in spans(b):
                    if hh == h:
                        part[b, 0, t // 2, r0 : r0 + n] = out[j * n : (j + 1) * n, :share]
                        part[b, 1, t // 2, r0 : r0 + n] = out[j * n : (j + 1) * n, share:]
        core_copy(b).start()

    def x_copy(b, i):
        rows = pl.ds(0, rows_of[b])
        return send(psend.at[b, i, rows], precv.at[b, i, rows], xsem.at[b, i], x_to[i])

    def pair_sum(b):
        core_copy(b).wait_recv()
        for i in [*range(1, nx), 0]:
            to = lax.rem(x + i, nx)
            rows = slice(0, rows_of[b])
            total = part[b, c, to, rows].astype(F32) + pin[b, to, rows].astype(F32)
            psend[b, i, rows] = total.astype(BF16)
            if i > 0:
                x_copy(b, i).start()

    def strip(b, t):
        return hg.at[b, pl.ds(0, rows_of[b]), pl.ds(pl.multiple_of(t * share, share), share)]

    def own_strip(b):
        return hgown.at[b, pl.ds(0, rows_of[b])]

    def hg_x(b, i):
        return send(own_strip(b), strip(b, tp), hxsem.at[b, i], x_to[i])

    def hg_core(b, i):
        t = lax.rem(x + nx - i, nx) * 2 + c
        return send(own_strip(b) if i == 0 else strip(b, t), strip(b, t), hcsem.at[b, i], other)

    def hg_keep(b):
        return pltpu.make_async_copy(own_strip(b), strip(b, tp), lsem.at[b])

    def middle(b):
        rows, block = rows_of[b], blocks_of[b]
        hidden = psend[b, 0, :rows].astype(F32)
        for i in range(1, nx):
            x_copy(b, i).wait_recv()
            hidden = hidden + precv[b, i, :rows].astype(F32)
        sig = jax.nn.sigmoid(hidden)
        row_grad = xin[b, :rows, feat:].astype(F32)
        hgown[b, :rows] = (row_grad * (sig * (1.0 + hidden * (1.0 - sig)))).astype(BF16)
        for i in range(1, nx):
            hg_x(b, i).start()
        hg_core(b, 0).start()
        hg_keep(b).start()
        acts = (hidden * sig).astype(BF16)
        act[b, :rows] = acts
        aret[b, 0:block] = acts[0:block]
        for copy in y_copies(b, asem, act, aret, y_back):
            copy.start()

    def hg_forward(b):
        for i in range(1, nx):
            hg_x(b, i).wait_recv()
            hg_core(b, i).start()

    def mix(b):
        for copy in y_copies(b, asem, act, aret, y_back):
            copy.wait_recv()
        nslot, rows = SIZES[b], rows_of[b]
        acts = aret[b, :rows].astype(F32)
        weighted = (gatec[b, :rows] * acts).astype(BF16)
        pmix[groups(b)] = dot(pmat[b, :rows, : nslot * count], weighted, 0, 0).astype(BF16)
        high, low = two_parts(acts * graw[b, :rows].astype(F32))
        ones = jnp.ones((8, share), BF16)
        sums = []
        for j, h, r0, n in spans(b):
            line = dot(ones, high[r0 : r0 + n], 1, 1) + dot(ones, low[r0 : r0 + n], 1, 1)
            line_high, line_low = two_parts(line)
            spread = pmat[b, r0 : r0 + n, : nslot * count]
            sums.append((2 * j + h, dot(line_high, spread) + dot(line_low, spread)))
        for g in range(nslot):
            named = inf[first_slot[b] + g, :topk]
            out = jnp.zeros((topk, count), F32)
            for e, value in sums:
                here = value[:topk, g * count : (g + 1) * count]
                out = out + jnp.where(named == eid[e : e + 1], here, 0.0)
            pgg[first_slot[b] + g] = out

    def backward(b):
        hg_keep(b).wait()
        for i in range(nx):
            hg_core(b, i).wait_recv()
        for h in range(2):
            out = dot(blocks(hg, b, h), wsel[h], 1, 1).astype(BF16)
            for j, hh, r0, n in spans(b):
                if hh == h:
                    (rret if j == 0 else brow)[b, r0 : r0 + n] = out[j * n : (j + 1) * n]
        for copy in y_copies(b, bsem, brow, rret, y_back):
            copy.start()

    def scatter(b):
        for copy in y_copies(b, bsem, brow, rret, y_back):
            copy.wait_recv()
        rows = rows_of[b]
        pick = pmat[b, :rows, : SIZES[b] * count]
        ptok[groups(b)] = dot(pick, rret[b, :rows], 0, 0).astype(BF16)

    def weight_grad(k):
        wide = ff // 4
        cols = slice(k * wide, (k + 1) * wide)
        sums = []
        for h in range(2):
            left = jnp.concatenate([blocks(xin, b, h, slice(0, feat)) for b in range(BATCHES)], 0)
            right = jnp.concatenate([blocks(hg, b, h, cols) for b in range(BATCHES)], 0)
            sums.append(dot(left, right, 0, 0))
        flip = swap(sums[0].shape)
        gup[0, :, cols] = jnp.where(flip, sums[1], sums[0]).astype(BF16)
        gup[1, :, cols] = jnp.where(flip, sums[0], sums[1]).astype(BF16)

    def rs_copy(way, d, q):
        src = pos(sign[1 - way] * d) * count + q * quarter
        return send(
            ptok.at[pl.ds(src, quarter)], rs.at[way, d - 1, pl.ds(q * quarter, quarter)],
            rsem.at[way, d - 1, q], z_to[way],
        )

    def rs_has(way, d, q):
        return d < half or (d == half and q // 2 == 1 - way)

    pieces = [(way, q) for p in range(2) for way, q in ((1, p), (0, 2 + p))]
    pieces = pieces + [(1 - way, q) for way, q in pieces]

    def rs_start():
        for way, q in pieces:
            if rs_has(way, half, q):
                rs_copy(way, half, q).start()
        for way, q in pieces:
            if not rs_has(way, half, q):
                rs_copy(way, half - 1, q).start()

    def rs_step(d):
        for way, q in pieces[4:] + pieces[:4]:
            if not rs_has(way, d + 1, q):
                continue
            rs_copy(way, d + 1, q).wait_recv()
            at = pos(sign[1 - way] * d) * count + q * quarter
            arrived = rs[way, d, q * quarter : (q + 1) * quarter].astype(F32)
            ptok[at : at + quarter] = (ptok[at : at + quarter].astype(F32) + arrived).astype(BF16)
            rs_copy(way, d, q).start()

    def rs_end():
        for q in range(4):
            total = ptok[mine + q * quarter : mine + (q + 1) * quarter].astype(F32)
            for way in (1, 0):
                rs_copy(way, 1, q).wait_recv()
                total = total + rs[way, 0, q * quarter : (q + 1) * quarter].astype(F32)
            gtok_ref[q * quarter : (q + 1) * quarter] = total.astype(BF16)

    def ms_copy(way, d):
        src = pos(sign[1 - way] * d)
        return send(
            pmix.at[pl.ds(src * count, count)], ms.at[way, d - 1], msem.at[way, d - 1], z_to[way]
        )

    def gs_copy(way, d):
        src = pos(sign[1 - way] * d)
        return send(pgg.at[src], gs.at[way, d - 1], gsem.at[way, d - 1], z_to[way])

    def ms_has(way, d):
        return d < half or (d == half and way == 1)

    def ms_step(d):
        for way in (1, 0):
            if not ms_has(way, d):
                continue
            if ms_has(way, d + 1):
                src = pos(sign[1 - way] * d)
                ms_copy(way, d + 1).wait_recv()
                at = slice(src * count, (src + 1) * count)
                pmix[at] = (pmix[at].astype(F32) + ms[way, d].astype(F32)).astype(BF16)
                gs_copy(way, d + 1).wait_recv()
                pgg[src] = pgg[src] + gs[way, d]
            ms_copy(way, d).start()
            gs_copy(way, d).start()

    def tx_core():
        return send(gx.at[0], gx.at[1], txsem.at[0], other)

    def tx_copy(i):
        return send(gx.at[2], gx.at[2 + i], txsem.at[i], x_to[i])

    def ms_end():
        total = pmix[mine : mine + count].astype(F32)
        gates = pgg[pos(0)]
        for way in (1, 0):
            ms_copy(way, 1).wait_recv()
            total = total + ms[way, 0].astype(F32)
            gs_copy(way, 1).wait_recv()
            gates = gates + gs[way, 0]
        mixed_ref[...] = total.astype(BF16)
        gx[0] = gates
        tx_core().start()

    def tx_middle():
        tx_core().wait_recv()
        gx[2] = gx[0] + gx[1]
        for i in range(1, nx):
            tx_copy(i).start()

    def tx_end():
        total = gx[2]
        for i in range(1, nx):
            tx_copy(i).wait_recv()
            total = total + gx[2 + i]
        ggate_ref[...] = total

    def order_weights():
        load.wait()
        for k in range(4):
            cols = slice(k * (ff // 4), (k + 1) * (ff // 4))
            first, second = wraw[0, :, cols].astype(F32), wraw[1, :, cols].astype(F32)
            flip = swap(first.shape)
            wsel[0, :, cols] = jnp.where(flip, second, first).astype(BF16)
            wsel[1, :, cols] = jnp.where(flip, first, second).astype(BF16)

    stage = {
        "g": gather, "f": forward, "p": pair_sum, "m": middle, "h": hg_forward, "x": mix,
        "b": backward, "s": scatter, "w": weight_grad, "M": ms_step, "R": rs_step,
    }

    def run(jobs):
        for job in jobs.split():
            stage[job[0]](int(job[1:]))

    ag_start()
    order_weights()
    for s in range(1, half + 1):
        for q in range(4):
            ag_step(s, q)
            run(DURING.get((s, q), ""))
    run(BETWEEN)
    rs_start()
    run("s2 R7 M4 R6 M3 R5 M2 w0 R4 M1 w1 R3")
    ms_end()
    run("w2 R2")
    tx_middle()
    run("w3")
    tx_end()
    store = pltpu.make_async_copy(gup, gup_hbm, osem)
    store.start()
    run("R1")
    rs_end()
    store.wait()

    for s in range(1, half + 1):
        for way in (0, 1):
            for q in range(4):
                if ag_has(way, s, q):
                    ag_copy(way, s, q).wait_send()
            if ag_info_has(way, s):
                ag_info(way, s).wait_send()
    for d in range(1, half + 1):
        for way, q in pieces:
            if rs_has(way, d, q):
                rs_copy(way, d, q).wait_send()
        for way in (0, 1):
            if ms_has(way, d):
                ms_copy(way, d).wait_send()
                gs_copy(way, d).wait_send()
    for b in range(BATCHES):
        for copy in y_copies(b, ysem, xsend, xin, y_to):
            copy.wait_send()
        for copy in y_copies(b, asem, act, aret, y_back):
            copy.wait_send()
        for copy in y_copies(b, bsem, brow, rret, y_back):
            copy.wait_send()
        core_copy(b).wait_send()
        for i in range(nx):
            hg_core(b, i).wait_send()
            if i > 0:
                x_copy(b, i).wait_send()
                hg_x(b, i).wait_send()
    tx_core().wait_send()
    for i in range(1, nx):
        tx_copy(i).wait_send()


def copy_kernel(*refs):
    count = (len(refs) - 1) // 3
    sources, targets, held, sems = refs[:count], refs[count : 2 * count], refs[2 * count : -1], refs[-1]
    pieces = []
    for k in range(count):
        depth = sources[k].shape[0]
        cuts = PIECES if depth % (16 * PIECES) == 0 and depth > 128 else 1
        for i in range(cuts):
            rows = pl.ds(i * (depth // cuts), depth // cuts)
            pieces.append((sources[k].at[rows], held[k].at[rows], targets[k].at[rows]))
    loads = [pltpu.make_async_copy(a, b, sems.at[0, i]) for i, (a, b, c) in enumerate(pieces)]
    stores = [pltpu.make_async_copy(b, c, sems.at[1, i]) for i, (a, b, c) in enumerate(pieces)]
    for load in loads:
        load.start()
    for load, store in zip(loads, stores):
        load.wait()
        store.start()
    for store in stores:
        store.wait()


def on_device(ny, tokens, routes, gates, up_weight, replica_on, grad_out):
    count, feat = tokens.shape
    topk = routes.shape[1]
    share = grad_out.shape[1]
    ff = up_weight.shape[2]
    experts = replica_on.shape[0]
    nz = lax.axis_size("ep") // ny
    nx = lax.axis_size("tp") // 2
    half = nz // 2
    rows = ny * sum(block_rows(max(SIZES)))
    slots = max(SIZES) * count
    vmem = pl.BlockSpec(memory_space=pltpu.VMEM)
    hbm = pl.BlockSpec(memory_space=pl.ANY)

    def dma(*shape):
        return pltpu.SemaphoreType.DMA(shape + (2,))

    out_shape = [
        jax.ShapeDtypeStruct((count, share), BF16),
        jax.ShapeDtypeStruct((count, feat), BF16),
        jax.ShapeDtypeStruct((topk, count), F32),
        jax.ShapeDtypeStruct(up_weight.shape, BF16),
    ]
    outs = pl.pallas_call(
        functools.partial(kernel, (ny, nz, nx)),
        out_shape=out_shape,
        in_specs=[vmem] * 5 + [hbm],
        out_specs=[vmem] * 3 + [hbm],
        scratch_shapes=[
            pltpu.VMEM((2 * ny, count), F32),
            pltpu.VMEM((2 * ny, count), F32),
            pltpu.VMEM((nz * count, feat + share), BF16),
            pltpu.VMEM((nz, 2 * topk, count), F32),
            pltpu.VMEM(up_weight.shape, BF16),
            pltpu.VMEM(up_weight.shape, BF16),
            pltpu.VMEM((BATCHES, rows, slots), BF16),
            pltpu.VMEM((BATCHES, rows, share), F32),
            pltpu.VMEM((BATCHES, rows, share), BF16),
            pltpu.VMEM((BATCHES, rows, feat + share), BF16),
            pltpu.VMEM((BATCHES, rows, feat + share), BF16),
            pltpu.VMEM((BATCHES, 2, nx, rows, share), BF16),
            pltpu.VMEM((BATCHES, nx, rows, share), BF16),
            pltpu.VMEM((BATCHES, nx, rows, share), BF16),
            pltpu.VMEM((BATCHES, nx, rows, share), BF16),
            pltpu.VMEM((BATCHES, rows, share), BF16),
            pltpu.VMEM((BATCHES, rows, share), BF16),
            pltpu.VMEM((BATCHES, rows, share), BF16),
            pltpu.VMEM((BATCHES, rows, ff), BF16),
            pltpu.VMEM((BATCHES, rows, feat), BF16),
            pltpu.VMEM((BATCHES, rows, feat), BF16),
            pltpu.VMEM((nz * count, feat), BF16),
            pltpu.VMEM((2, half, count, feat), BF16),
            pltpu.VMEM((nz * count, share), BF16),
            pltpu.VMEM((2, half, count, share), BF16),
            pltpu.VMEM((nz, topk, count), F32),
            pltpu.VMEM((2, half, topk, count), F32),
            pltpu.VMEM(up_weight.shape, BF16),
            pltpu.VMEM((2 + nx, topk, count), F32),
            pltpu.SemaphoreType.DMA,
            pltpu.SemaphoreType.DMA,
            pltpu.SemaphoreType.DMA((BATCHES,)),
            dma(2, half, 4),
            dma(2, half),
            dma(BATCHES, ny),
            dma(BATCHES),
            dma(BATCHES, nx),
            dma(BATCHES, ny),
            dma(BATCHES, nx),
            dma(BATCHES, nx),
            dma(BATCHES, ny),
            dma(2, half, 4),
            dma(2, half),
            dma(2, half),
            dma(nx),
        ],
        compiler_params=pltpu.CompilerParams(
            collective_id=0, has_side_effects=True, vmem_limit_bytes=56 * 1024 * 1024
        ),
        cost_estimate=pl.CostEstimate(
            flops=32 * rows * feat * ff, bytes_accessed=8 * feat * ff, transcendentals=8 * rows * share
        ),
    )(routes.T, gates.T, replica_on[None, :], tokens, grad_out, up_weight)
    flat = jax.ShapeDtypeStruct((up_weight.shape[0] * feat, ff), BF16)
    out_shape = [*out_shape[:3], flat]
    mixed, gtok, ggate, gup = pl.pallas_call(
        copy_kernel,
        out_shape=out_shape,
        in_specs=[hbm] * 4,
        out_specs=[hbm] * 4,
        scratch_shapes=[pltpu.VMEM(o.shape, o.dtype) for o in out_shape]
        + [pltpu.SemaphoreType.DMA((2, 3 + PIECES))],
        compiler_params=pltpu.CompilerParams(vmem_limit_bytes=16 * 1024 * 1024),
    )(*outs[:3], outs[3].reshape(flat.shape))
    gup = gup.reshape(up_weight.shape)
    return mixed, gtok, ggate.T, gup


def solution(mesh, ny=NY):
    return jax.shard_map(
        functools.partial(on_device, ny),
        mesh=mesh,
        in_specs=(
            P("ep", "tp"), P("ep", None), P("ep", None), P("ep", "tp", None), P(), P("ep", "tp"),
        ),
        out_specs=(P("ep", "tp"), P("ep", "tp"), P("ep", None), P("ep", "tp", None)),
        check_vma=False,
    )
```

```python
import functools

import jax
import jax.numpy as jnp
from jax import lax
from jax.experimental import pallas as pl
from jax.experimental.pallas import tpu as pltpu
from jax.sharding import PartitionSpec as P

MESH = pl.DeviceIdType.MESH
CAP = 6
CAPS = (2 * CAP, CAP)
NY = 4
PIECES = 8
SIZES = (4, 4, 4, 2, 2)
BATCHES = len(SIZES)
BF16, F32 = jnp.bfloat16, jnp.float32


def dot(a, b, ca=1, cb=0):
    return lax.dot_general(a, b, (((ca,), (cb,)), ((), ())), preferred_element_type=F32)


def two_parts(value):
    high = value.astype(BF16)
    return high, (value - high.astype(F32)).astype(BF16)


def slot_order(nz):
    order = [0]
    for far in range(1, nz // 2):
        order += [far, nz - far]
    return order + [nz // 2]


def block_rows(nslot):
    return tuple(-(-cap * nslot // 16) * 16 for cap in CAPS)


DURING = {
    (2, 3): "g0", (4, 3): "g1 f0", (5, 1): "p0", (6, 3): "g2 m0", (7, 0): "f1", (7, 2): "p1",
    (7, 3): "g3", (8, 3): "g4",
}
BETWEEN = (
    "f3 f2 p3 p2 h0 x0 b0 A0 f4 p4 m3 s0 m4 m2 h3 x3 b3 m1 x4 M8 h4 M7 b4 h2 x2 s3 b2 M6 s4"
)


def kernel(
    dims,
    routes_ref, gates_ref, rep_ref, tokens_ref, grad_ref, weight_hbm,
    mixed_ref, gtok_ref, ggate_ref, gup_hbm,
    eid, hot, ring, inf, wraw, wsel, pmat, gatec, graw, xsend, xin, part, pin, psend, precv,
    act, aret, hgown, hg, brow, rret, ptok, rs, pmix, ms, pgg, gs, gup, gx,
    wsem, osem, lsem, ag, agi, ysem, csem, xsem, asem, hxsem, hcsem, bsem, rsem, msem, gsem, txsem,
):
    ny, nz, nx = dims
    count, feat = tokens_ref.shape
    topk = routes_ref.shape[0]
    experts = rep_ref.shape[1]
    share = grad_ref.shape[1]
    ff = wsel.shape[2]
    half = nz // 2
    order = slot_order(nz)
    first_slot = [sum(SIZES[:b]) for b in range(BATCHES)]
    pads = [block_rows(size) for size in SIZES]
    blocks_of = [sum(pad) for pad in pads]
    rows_of = [ny * block for block in blocks_of]

    def spans(b):
        return [
            (j, h, j * blocks_of[b] + h * pads[b][0], pads[b][h]) for j in range(ny) for h in range(2)
        ]

    def groups(b):
        return slice(first_slot[b] * count, (first_slot[b] + SIZES[b]) * count)

    quarter = count // 4

    ep, tp = lax.axis_index("ep"), lax.axis_index("tp")
    y, z = lax.div(ep, nz), lax.rem(ep, nz)
    x, c = lax.div(tp, 2), lax.rem(tp, 2)

    def device(yy, zz, xx, cc):
        return (lax.rem(yy, ny) * nz + lax.rem(zz, nz), lax.rem(xx, nx) * 2 + cc)

    z_to = (device(y, z + nz - 1, x, c), device(y, z + 1, x, c))
    y_to = [device(y + j, z, x, c) for j in range(ny)]
    y_back = [device(y + ny - j, z, x, c) for j in range(ny)]
    x_to = [device(y, z, x + i, c) for i in range(nx)]
    other = device(y, z, x, 1 - c)

    def pos(d):
        return order.index(d % nz)

    def send(src, dst, sems, to):
        return pltpu.make_async_remote_copy(
            src_ref=src, dst_ref=dst, send_sem=sems.at[0], recv_sem=sems.at[1],
            device_id=to, device_id_type=MESH,
        )

    load = pltpu.make_async_copy(weight_hbm, wraw, wsem)
    load.start()
    barrier = pltpu.get_barrier_semaphore()
    partners = list(z_to) + y_to[1:] + x_to[1:] + [other]
    for partner in partners:
        pl.semaphore_signal(barrier, inc=1, device_id=partner, device_id_type=MESH)

    mine = pos(0) * count
    ring[mine : mine + count, :feat] = tokens_ref[...]
    ring[mine : mine + count, feat:] = grad_ref[...]
    inf[pos(0), :topk] = routes_ref[...].astype(F32)
    inf[pos(0), topk:] = gates_ref[...]

    def homes(width):
        line = lax.broadcasted_iota(jnp.int32, (2 * ny, width), 0)
        return line, lax.rem(y + lax.shift_right_logical(line, 1), ny) * nz + z

    line, home = homes(experts)
    at = lax.broadcasted_iota(jnp.int32, (2 * ny, experts), 1) == 2 * home + 1
    second = jnp.sum(jnp.where(at, rep_ref[...].astype(F32), 0.0), 1, keepdims=True)
    line, home = homes(count)
    second = jnp.broadcast_to(second, (2 * ny, count))
    eid[...] = 2.0 * home.astype(F32) + jnp.where(lax.rem(line, 2) == 0, second, 1.0 - second)
    hot[...] = second

    def swap(shape):
        return jnp.broadcast_to(hot[0:1, 0:1], shape) > 0.0

    pl.semaphore_wait(barrier, len(partners))

    sign = (1, -1)

    def ag_copy(way, s, q):
        src, dst = pos(sign[way] * (s - 1)) * count, pos(sign[way] * s) * count
        return send(
            ring.at[pl.ds(src + q * quarter, quarter)], ring.at[pl.ds(dst + q * quarter, quarter)],
            ag.at[way, s - 1, q], z_to[way],
        )

    def ag_has(way, s, q):
        return s < half or (s == half and q // 2 == way)

    def ag_info(way, s):
        src, dst = pos(sign[way] * (s - 1)), pos(sign[way] * s)
        return send(inf.at[src], inf.at[dst], agi.at[way, s - 1], z_to[way])

    def ag_info_has(way, s):
        return s < half or (s == half and way == 0)

    def ag_start():
        for q in range(4):
            for way in (0, 1):
                ag_copy(way, 1, q).start()
                if q == 0:
                    ag_info(way, 1).start()

    def ag_step(s, q):
        for way in (0, 1):
            if ag_has(way, s, q):
                ag_copy(way, s, q).wait_recv()
                if ag_has(way, s + 1, q):
                    ag_copy(way, s + 1, q).start()
            if q == 0 and ag_info_has(way, s):
                ag_info(way, s).wait_recv()
                if ag_info_has(way, s + 1):
                    ag_info(way, s + 1).start()

    def blocks(ref, b, h, cols=slice(None)):
        return jnp.concatenate([ref[b, r0 : r0 + n, cols] for j, hh, r0, n in spans(b) if hh == h], 0)

    def y_copies(b, sems, src, dst, to):
        block = blocks_of[b]
        return [
            send(
                src.at[b, pl.ds(j * block, block)], dst.at[b, pl.ds(j * block, block)],
                sems.at[b, j], to[j],
            )
            for j in sorted(range(1, ny), key=lambda j: -min(j, ny - j))
        ]

    def gather(b):
        nslot, rows, block = SIZES[b], rows_of[b], blocks_of[b]
        eids = eid[...]
        caps = lax.rem(lax.broadcasted_iota(jnp.int32, eids.shape, 0), 2) == 0
        caps = jnp.where(caps, float(CAPS[0]), float(CAPS[1]))
        names, gate_of = [], []
        for g in range(nslot):
            named = jnp.zeros(eids.shape, F32)
            gated = jnp.zeros(eids.shape, F32)
            routing = inf[first_slot[b] + g]
            for k in range(topk):
                hit = routing[k : k + 1] == eids
                named = named + jnp.where(hit, 1.0, 0.0)
                gated = gated + jnp.where(hit, routing[topk + k : topk + k + 1], 0.0)
            names.append(named)
            gate_of.append(gated)
        upper = (
            lax.broadcasted_iota(jnp.int32, (count, count), 0)
            < lax.broadcasted_iota(jnp.int32, (count, count), 1)
        ).astype(BF16)
        rank = dot(jnp.concatenate(names, 0).astype(BF16), upper)
        place = []
        for g in range(nslot):
            r = rank[g * 2 * ny : (g + 1) * 2 * ny]
            place.append(jnp.where((names[g] > 0.0) & (r < caps), r + g * caps, -1.0))
        place = jnp.concatenate(place, 1)
        gate_of = jnp.concatenate(gate_of, 1)
        for j, h, r0, n in spans(b):
            e = 2 * j + h
            row = lax.broadcasted_iota(jnp.int32, (n, nslot * count), 0).astype(F32)
            hit = row == place[e : e + 1]
            pmat[b, r0 : r0 + n, : nslot * count] = jnp.where(hit, 1.0, 0.0).astype(BF16)
            gate = jnp.sum(jnp.where(hit, gate_of[e : e + 1], 0.0), 1, keepdims=True)
            gatec[b, r0 : r0 + n] = jnp.broadcast_to(gate, (n, share))
        pick = pmat[b, :rows, : nslot * count]
        for c0 in range(0, feat, min(256, feat)):
            cols = slice(c0, c0 + min(256, feat))
            got = dot(pick, ring[groups(b), cols]).astype(BF16)
            xsend[b, :rows, cols] = got
            xin[b, 0:block, cols] = got[0:block]
        got = dot(pick, ring[groups(b), feat:])
        graw[b, :rows] = got.astype(BF16)
        row_grad = (gatec[b, :rows] * got).astype(BF16)
        xsend[b, :rows, feat:] = row_grad
        xin[b, 0:block, feat:] = row_grad[0:block]
        for copy in y_copies(b, ysem, xsend, xin, y_to):
            copy.start()

    def core_copy(b):
        rows = pl.ds(0, rows_of[b])
        return send(part.at[b, 1 - c, :, rows], pin.at[b, :, rows], csem.at[b], other)

    def forward(b):
        for copy in y_copies(b, ysem, xsend, xin, y_to):
            copy.wait_recv()
        for h in range(2):
            rows_in = blocks(xin, b, h, slice(0, feat))
            for t in range(0, ff // share, 2):
                out = dot(rows_in, wsel[h, :, t * share : (t + 2) * share]).astype(BF16)
                for j, hh, r0, n in spans(b):
                    if hh == h:
                        part[b, 0, t // 2, r0 : r0 + n] = out[j * n : (j + 1) * n, :share]
                        part[b, 1, t // 2, r0 : r0 + n] = out[j * n : (j + 1) * n, share:]
        core_copy(b).start()

    def x_copy(b, i):
        rows = pl.ds(0, rows_of[b])
        return send(psend.at[b, i, rows], precv.at[b, i, rows], xsem.at[b, i], x_to[i])

    def pair_sum(b):
        core_copy(b).wait_recv()
        for i in [*sorted(range(1, nx), key=lambda i: -min(i, nx - i)), 0]:
            to = lax.rem(x + i, nx)
            rows = slice(0, rows_of[b])
            total = part[b, c, to, rows].astype(F32) + pin[b, to, rows].astype(F32)
            psend[b, i, rows] = total.astype(BF16)
            if i > 0:
                x_copy(b, i).start()

    def strip(b, t):
        return hg.at[b, pl.ds(0, rows_of[b]), pl.ds(pl.multiple_of(t * share, share), share)]

    def own_strip(b):
        return hgown.at[b, pl.ds(0, rows_of[b])]

    def hg_x(b, i):
        return send(own_strip(b), strip(b, tp), hxsem.at[b, i], x_to[i])

    def hg_core(b, i):
        t = lax.rem(x + nx - i, nx) * 2 + c
        return send(own_strip(b) if i == 0 else strip(b, t), strip(b, t), hcsem.at[b, i], other)

    def hg_keep(b):
        return pltpu.make_async_copy(own_strip(b), strip(b, tp), lsem.at[b])

    def middle(b):
        rows, block = rows_of[b], blocks_of[b]
        hidden = psend[b, 0, :rows].astype(F32)
        for i in range(1, nx):
            x_copy(b, i).wait_recv()
            hidden = hidden + precv[b, i, :rows].astype(F32)
        sig = jax.nn.sigmoid(hidden)
        row_grad = xin[b, :rows, feat:].astype(F32)
        hgown[b, :rows] = (row_grad * (sig * (1.0 + hidden * (1.0 - sig)))).astype(BF16)
        for i in range(1, nx):
            hg_x(b, i).start()
        hg_core(b, 0).start()
        hg_keep(b).start()
        acts = (hidden * sig).astype(BF16)
        act[b, :rows] = acts
        aret[b, 0:block] = acts[0:block]
        for copy in y_copies(b, asem, act, aret, y_back):
            copy.start()

    def hg_forward(b):
        for i in range(1, nx):
            hg_x(b, i).wait_recv()
            hg_core(b, i).start()

    def mix(b):
        for copy in y_copies(b, asem, act, aret, y_back):
            copy.wait_recv()
        nslot, rows = SIZES[b], rows_of[b]
        acts = aret[b, :rows].astype(F32)
        weighted = (gatec[b, :rows] * acts).astype(BF16)
        pmix[groups(b)] = dot(pmat[b, :rows, : nslot * count], weighted, 0, 0).astype(BF16)
        high, low = two_parts(acts * graw[b, :rows].astype(F32))
        ones = jnp.ones((8, share), BF16)
        sums = []
        for j, h, r0, n in spans(b):
            line = dot(ones, high[r0 : r0 + n], 1, 1) + dot(ones, low[r0 : r0 + n], 1, 1)
            line_high, line_low = two_parts(line)
            spread = pmat[b, r0 : r0 + n, : nslot * count]
            sums.append((2 * j + h, dot(line_high, spread) + dot(line_low, spread)))
        for g in range(nslot):
            named = inf[first_slot[b] + g, :topk]
            out = jnp.zeros((topk, count), F32)
            for e, value in sums:
                here = value[:topk, g * count : (g + 1) * count]
                out = out + jnp.where(named == eid[e : e + 1], here, 0.0)
            pgg[first_slot[b] + g] = out

    def backward(b):
        hg_keep(b).wait()
        for i in range(nx):
            hg_core(b, i).wait_recv()
        for h in range(2):
            out = dot(blocks(hg, b, h), wsel[h], 1, 1).astype(BF16)
            for j, hh, r0, n in spans(b):
                if hh == h:
                    (rret if j == 0 else brow)[b, r0 : r0 + n] = out[j * n : (j + 1) * n]
        for copy in y_copies(b, bsem, brow, rret, y_back):
            copy.start()

    def scatter(b):
        for copy in y_copies(b, bsem, brow, rret, y_back):
            copy.wait_recv()
        rows = rows_of[b]
        pick = pmat[b, :rows, : SIZES[b] * count]
        ptok[groups(b)] = dot(pick, rret[b, :rows], 0, 0).astype(BF16)

    def weight_grad(k):
        wide = ff // 4
        cols = slice(k * wide, (k + 1) * wide)
        sums = []
        for h in range(2):
            left = jnp.concatenate([blocks(xin, b, h, slice(0, feat)) for b in range(BATCHES)], 0)
            right = jnp.concatenate([blocks(hg, b, h, cols) for b in range(BATCHES)], 0)
            sums.append(dot(left, right, 0, 0))
        flip = swap(sums[0].shape)
        gup[0, :, cols] = jnp.where(flip, sums[1], sums[0]).astype(BF16)
        gup[1, :, cols] = jnp.where(flip, sums[0], sums[1]).astype(BF16)

    def rs_copy(way, d, q):
        src = pos(sign[1 - way] * d) * count + q * quarter
        return send(
            ptok.at[pl.ds(src, quarter)], rs.at[way, d - 1, pl.ds(q * quarter, quarter)],
            rsem.at[way, d - 1, q], z_to[way],
        )

    def rs_has(way, d, q):
        return d < half or (d == half and q // 2 == 1 - way)

    pieces = [(way, q) for p in range(2) for way, q in ((1, p), (0, 2 + p))]
    pieces = pieces + [(1 - way, q) for way, q in pieces]

    def rs_start():
        for way, q in pieces:
            if rs_has(way, half, q):
                rs_copy(way, half, q).start()
        for way, q in pieces:
            if not rs_has(way, half, q):
                rs_copy(way, half - 1, q).start()

    def rs_step(d):
        for way, q in pieces[4:] + pieces[:4]:
            if not rs_has(way, d + 1, q):
                continue
            rs_copy(way, d + 1, q).wait_recv()
            at = pos(sign[1 - way] * d) * count + q * quarter
            arrived = rs[way, d, q * quarter : (q + 1) * quarter].astype(F32)
            ptok[at : at + quarter] = (ptok[at : at + quarter].astype(F32) + arrived).astype(BF16)
            rs_copy(way, d, q).start()

    def rs_end():
        for q in range(4):
            total = ptok[mine + q * quarter : mine + (q + 1) * quarter].astype(F32)
            for way in (1, 0):
                rs_copy(way, 1, q).wait_recv()
                total = total + rs[way, 0, q * quarter : (q + 1) * quarter].astype(F32)
            gtok_ref[q * quarter : (q + 1) * quarter] = total.astype(BF16)

    def ms_copy(way, d):
        src = pos(sign[1 - way] * d)
        return send(
            pmix.at[pl.ds(src * count, count)], ms.at[way, d - 1], msem.at[way, d - 1], z_to[way]
        )

    def gs_copy(way, d):
        src = pos(sign[1 - way] * d)
        return send(pgg.at[src], gs.at[way, d - 1], gsem.at[way, d - 1], z_to[way])

    def ms_has(way, d):
        return d < half or (d == half and way == 1)

    def ms_step(d):
        for way in (1, 0):
            if not ms_has(way, d):
                continue
            if ms_has(way, d + 1):
                src = pos(sign[1 - way] * d)
                ms_copy(way, d + 1).wait_recv()
                at = slice(src * count, (src + 1) * count)
                pmix[at] = (pmix[at].astype(F32) + ms[way, d].astype(F32)).astype(BF16)
                gs_copy(way, d + 1).wait_recv()
                pgg[src] = pgg[src] + gs[way, d]
            ms_copy(way, d).start()
            gs_copy(way, d).start()

    def tx_core():
        return send(gx.at[0], gx.at[1], txsem.at[0], other)

    def tx_copy(i):
        return send(gx.at[2], gx.at[2 + i], txsem.at[i], x_to[i])

    def ms_end():
        total = pmix[mine : mine + count].astype(F32)
        gates = pgg[pos(0)]
        for way in (1, 0):
            ms_copy(way, 1).wait_recv()
            total = total + ms[way, 0].astype(F32)
            gs_copy(way, 1).wait_recv()
            gates = gates + gs[way, 0]
        mixed_ref[...] = total.astype(BF16)
        gx[0] = gates
        tx_core().start()

    def tx_middle():
        tx_core().wait_recv()
        gx[2] = gx[0] + gx[1]
        for i in range(1, nx):
            tx_copy(i).start()

    def tx_end():
        total = gx[2]
        for i in range(1, nx):
            tx_copy(i).wait_recv()
            total = total + gx[2 + i]
        ggate_ref[...] = total

    def order_weights():
        load.wait()
        for k in range(4):
            cols = slice(k * (ff // 4), (k + 1) * (ff // 4))
            first, second = wraw[0, :, cols].astype(F32), wraw[1, :, cols].astype(F32)
            flip = swap(first.shape)
            wsel[0, :, cols] = jnp.where(flip, second, first).astype(BF16)
            wsel[1, :, cols] = jnp.where(flip, first, second).astype(BF16)

    def drain_gather(_):
        for s in range(1, half + 1):
            for way in (0, 1):
                for q in range(4):
                    if ag_has(way, s, q):
                        ag_copy(way, s, q).wait_send()
                if ag_info_has(way, s):
                    ag_info(way, s).wait_send()

    def drain_batch(b):
        for copy in y_copies(b, ysem, xsend, xin, y_to):
            copy.wait_send()
        for copy in y_copies(b, asem, act, aret, y_back):
            copy.wait_send()
        for copy in y_copies(b, bsem, brow, rret, y_back):
            copy.wait_send()
        core_copy(b).wait_send()
        for i in range(nx):
            hg_core(b, i).wait_send()
            if i > 0:
                x_copy(b, i).wait_send()
                hg_x(b, i).wait_send()

    def drain_sums(far):
        for d in far:
            for way, q in pieces:
                if rs_has(way, d, q):
                    rs_copy(way, d, q).wait_send()
            for way in (0, 1):
                if ms_has(way, d):
                    ms_copy(way, d).wait_send()
                    gs_copy(way, d).wait_send()

    stage = {
        "g": gather, "f": forward, "p": pair_sum, "m": middle, "h": hg_forward, "x": mix,
        "b": backward, "s": scatter, "w": weight_grad, "M": ms_step, "R": rs_step,
        "A": drain_gather, "D": drain_batch,
    }

    def run(jobs):
        for job in jobs.split():
            stage[job[0]](int(job[1:]))

    ag_start()
    order_weights()
    for s in range(1, half + 1):
        for q in range(4):
            ag_step(s, q)
            run(DURING.get((s, q), ""))
    run(BETWEEN)
    rs_start()
    run("h1 x1 b1 R7 s2 M5 R6 M4 R5 s1 M3 R4 M2 R3 M1")
    ms_end()
    run("w0 w1 R2")
    tx_middle()
    run("D0 w2 D1 D2 w3 D3 D4")
    tx_end()
    store = pltpu.make_async_copy(gup, gup_hbm, osem)
    store.start()
    run("R1")
    drain_sums(range(2, half + 1))
    rs_end()
    store.wait()

    drain_sums((1,))
    tx_core().wait_send()
    for i in range(1, nx):
        tx_copy(i).wait_send()


def copy_kernel(*refs):
    count = (len(refs) - 1) // 3
    sources, targets, held, sems = refs[:count], refs[count : 2 * count], refs[2 * count : -1], refs[-1]
    pieces = []
    for k in range(count):
        depth = sources[k].shape[0]
        cuts = PIECES if depth % (16 * PIECES) == 0 and depth > 128 else 1
        for i in range(cuts):
            rows = pl.ds(i * (depth // cuts), depth // cuts)
            pieces.append((sources[k].at[rows], held[k].at[rows], targets[k].at[rows]))
    loads = [pltpu.make_async_copy(a, b, sems.at[0, i]) for i, (a, b, c) in enumerate(pieces)]
    stores = [pltpu.make_async_copy(b, c, sems.at[1, i]) for i, (a, b, c) in enumerate(pieces)]
    for load in loads:
        load.start()
    for load, store in zip(loads, stores):
        load.wait()
        store.start()
    for store in stores:
        store.wait()


def on_device(ny, tokens, routes, gates, up_weight, replica_on, grad_out):
    count, feat = tokens.shape
    topk = routes.shape[1]
    share = grad_out.shape[1]
    ff = up_weight.shape[2]
    experts = replica_on.shape[0]
    nz = lax.axis_size("ep") // ny
    nx = lax.axis_size("tp") // 2
    half = nz // 2
    rows = ny * sum(block_rows(max(SIZES)))
    slots = max(SIZES) * count
    vmem = pl.BlockSpec(memory_space=pltpu.VMEM)
    hbm = pl.BlockSpec(memory_space=pl.ANY)

    def dma(*shape):
        return pltpu.SemaphoreType.DMA(shape + (2,))

    out_shape = [
        jax.ShapeDtypeStruct((count, share), BF16),
        jax.ShapeDtypeStruct((count, feat), BF16),
        jax.ShapeDtypeStruct((topk, count), F32),
        jax.ShapeDtypeStruct(up_weight.shape, BF16),
    ]
    outs = pl.pallas_call(
        functools.partial(kernel, (ny, nz, nx)),
        out_shape=out_shape,
        in_specs=[vmem] * 5 + [hbm],
        out_specs=[vmem] * 3 + [hbm],
        scratch_shapes=[
            pltpu.VMEM((2 * ny, count), F32),
            pltpu.VMEM((2 * ny, count), F32),
            pltpu.VMEM((nz * count, feat + share), BF16),
            pltpu.VMEM((nz, 2 * topk, count), F32),
            pltpu.VMEM(up_weight.shape, BF16),
            pltpu.VMEM(up_weight.shape, BF16),
            pltpu.VMEM((BATCHES, rows, slots), BF16),
            pltpu.VMEM((BATCHES, rows, share), F32),
            pltpu.VMEM((BATCHES, rows, share), BF16),
            pltpu.VMEM((BATCHES, rows, feat + share), BF16),
            pltpu.VMEM((BATCHES, rows, feat + share), BF16),
            pltpu.VMEM((BATCHES, 2, nx, rows, share), BF16),
            pltpu.VMEM((BATCHES, nx, rows, share), BF16),
            pltpu.VMEM((BATCHES, nx, rows, share), BF16),
            pltpu.VMEM((BATCHES, nx, rows, share), BF16),
            pltpu.VMEM((BATCHES, rows, share), BF16),
            pltpu.VMEM((BATCHES, rows, share), BF16),
            pltpu.VMEM((BATCHES, rows, share), BF16),
            pltpu.VMEM((BATCHES, rows, ff), BF16),
            pltpu.VMEM((BATCHES, rows, feat), BF16),
            pltpu.VMEM((BATCHES, rows, feat), BF16),
            pltpu.VMEM((nz * count, feat), BF16),
            pltpu.VMEM((2, half, count, feat), BF16),
            pltpu.VMEM((nz * count, share), BF16),
            pltpu.VMEM((2, half, count, share), BF16),
            pltpu.VMEM((nz, topk, count), F32),
            pltpu.VMEM((2, half, topk, count), F32),
            pltpu.VMEM(up_weight.shape, BF16),
            pltpu.VMEM((2 + nx, topk, count), F32),
            pltpu.SemaphoreType.DMA,
            pltpu.SemaphoreType.DMA,
            pltpu.SemaphoreType.DMA((BATCHES,)),
            dma(2, half, 4),
            dma(2, half),
            dma(BATCHES, ny),
            dma(BATCHES),
            dma(BATCHES, nx),
            dma(BATCHES, ny),
            dma(BATCHES, nx),
            dma(BATCHES, nx),
            dma(BATCHES, ny),
            dma(2, half, 4),
            dma(2, half),
            dma(2, half),
            dma(nx),
        ],
        compiler_params=pltpu.CompilerParams(
            collective_id=0, has_side_effects=True, vmem_limit_bytes=56 * 1024 * 1024
        ),
        cost_estimate=pl.CostEstimate(
            flops=32 * rows * feat * ff, bytes_accessed=8 * feat * ff, transcendentals=8 * rows * share
        ),
    )(routes.T, gates.T, replica_on[None, :], tokens, grad_out, up_weight)
    flat = jax.ShapeDtypeStruct((up_weight.shape[0] * feat, ff), BF16)
    out_shape = [*out_shape[:3], flat]
    mixed, gtok, ggate, gup = pl.pallas_call(
        copy_kernel,
        out_shape=out_shape,
        in_specs=[hbm] * 4,
        out_specs=[hbm] * 4,
        scratch_shapes=[pltpu.VMEM(o.shape, o.dtype) for o in out_shape]
        + [pltpu.SemaphoreType.DMA((2, 3 + PIECES))],
        compiler_params=pltpu.CompilerParams(vmem_limit_bytes=56 * 1024 * 1024),
    )(*outs[:3], outs[3].reshape(flat.shape))
    gup = gup.reshape(up_weight.shape)
    return mixed, gtok, ggate.T, gup


def solution(mesh, ny=NY):
    return jax.shard_map(
        functools.partial(on_device, ny),
        mesh=mesh,
        in_specs=(
            P("ep", "tp"), P("ep", None), P("ep", None), P("ep", "tp", None), P(), P("ep", "tp"),
        ),
        out_specs=(P("ep", "tp"), P("ep", "tp"), P("ep", None), P("ep", "tp", None)),
        check_vma=False,
    )
```
